32 devices in a mesh: groups: 2 (over y), dp: 4 (over x, core), tensor: 4 (over z).
Axes of the slice: x: 2, y: 2, z: 4, core: 2. Of those that a mesh axis runs over, the one named last changes fastest.
Arguments:
- inputs: bfloat16 [4096, 4096], P(('groups', 'dp'), 'tensor'), parts along dimension 0, may hold values from -6 to 6
- out_grads: bfloat16 [4096, 4096], P(('groups', 'dp'), 'tensor'), parts along dimension 0, may hold values from -6 to 6
- example_ids: int32 [8, 512], P(('groups', 'dp')), parts along dimension 0, may hold values from 0 to 15, never falling along the last dimension, each value on 1 to 64 neighbouring positions
- query_inputs: bfloat16 [2048, 4096], P(('groups', 'dp'), 'tensor'), parts along dimension 0, may hold values from -6 to 6
- query_grads: bfloat16 [2048, 4096], P(('groups', 'dp'), 'tensor'), parts along dimension 0, may hold values from -6 to 6
- query_ids: int32 [8, 256], P(('groups', 'dp')), parts along dimension 0, may hold values from 0 to 15, never falling along the last dimension, each value on 1 to 32 neighbouring positions
- w_gate: bfloat16 [4096, 14336], P('dp', 'tensor'), may hold values from -0.09375 to 0.09375
- w_up: bfloat16 [4096, 14336], P('dp', 'tensor'), may hold values from -0.09375 to 0.09375
- in_project: bfloat16 [64, 14336], P(None, 'tensor'), may hold values from -0.046875 to 0.046875
- out_project: bfloat16 [64, 4096], P(None, 'tensor'), may hold values from -0.09375 to 0.09375
Outputs:
- sketches: float32 [128, 4096], P(('groups', 'dp')), parts along dimension 0
- scores: float32 [128, 64], P(('groups', 'dp')), parts along dimension 0
The draws below stay inside these ranges and needn't reach their ends.
There are 2 independent parts, one for each index of `groups`. The reference program is written for one: setup_inputs(seed, part) draws one part's arguments, and reference() takes and returns one part's arrays. A program takes and returns all parts, laid end to end along the dimension named above; an argument that names none is the same for every part. Nothing has to cross between parts.
Inputs may be any that keep to these rules, and one draw needn't show every extreme that they name: `example_ids`: row k holds the tokens of index k of dp: 16 training examples of consecutive tokens, numbered in order from 0, each of 1 to 64 tokens. `query_ids`: row k holds the tokens of index k of dp: 16 queries of consecutive tokens, numbered in order from 0, each of 1 to 32 tokens.
All inputs are finite; a program needn't handle non-finite values.
Results may differ from the reference program's by a relative error of at most 0.004.
Values may be sent and summed in bfloat16 or wider, within the bound.
A program may use at most 192 MiB of HBM per device.

```python
import math
import jax
import jax.numpy as jnp
import numpy as np
from jax import lax

D = 4096
FF = 14336
R = 64
TOK_DEV = 512
QTOK_DEV = 256
EX_DEV = 16
QEX_DEV = 16
MOST = 64
QMOST = 32
TOKENS = 2048
QTOKENS = 1024
EXAMPLES = 64
QUERIES = 64
N_DP = 4


def level_of(key, extent, shards, smallest, high):
    gain = 1.0
    for axis_at, shards_of in shards:
        steps = jax.random.uniform(jax.random.fold_in(jax.random.fold_in(key, 6), axis_at), (shards_of,), jnp.float32, smallest / len(shards), high / len(shards))
        gain = gain * jnp.repeat(jnp.exp(steps), extent[axis_at] // shards_of).reshape((-1,) + (1,) * (len(extent) - 1 - axis_at))
    return gain


def split_up(count, total, limit, lean):
    portions = [(1 << 20) // math.isqrt(standing ** lean) + 1 for standing in range(2, count + 1)]
    spare, given = total - limit - (count - 1), [1] * (count - 1)
    while spare > 0:
        movable = [i for i in range(count - 1) if given[i] < limit]
        mass, left = sum([portions[i] for i in movable]), spare
        for i in movable:
            more = min(limit - given[i], max(1, left * portions[i] // mass), spare)
            given[i] = given[i] + more
            spare = spare - more
    return np.array([limit] + given)


def ragged(own_key, amount, total, reach, slope):
    if amount == 2:
        one = jax.random.randint(own_key, (), max(1, total - reach), min(reach, total - 1) + 1)
        return jnp.stack([one, total - one])
    lengths = jnp.asarray(split_up(amount, total, reach, slope), jnp.int32)
    pairs = (amount - 1) // 2
    giver, sink = lengths[1:1 + 2 * pairs:2], lengths[2:2 + 2 * pairs:2]
    margin = jnp.minimum(giver - 1, reach - sink)
    shifted = jax.random.randint(jax.random.fold_in(own_key, 1), (pairs,), 0, 1 << 20) % (margin + 1)
    lengths = lengths.at[1:1 + 2 * pairs:2].set(giver - shifted).at[2:2 + 2 * pairs:2].set(sink + shifted)
    return lengths[jax.random.permutation(jax.random.fold_in(own_key, 2), amount)]


def centred(own_key, extent, width, limit, cuts=(), kind=jnp.bfloat16):
    result = width * jax.random.normal(own_key, extent, jnp.float32)
    if cuts:
        result = result * level_of(own_key, extent, cuts, -0.22, 0.18)
    return jnp.clip(result, -limit, limit).astype(kind)


def setup_inputs(seed: int = 0, part: int = 0) -> dict:
    key_list = jax.random.split(jax.random.key(seed), 11)
    part_keys = jax.random.split(jax.random.fold_in(key_list[10], part), 11)
    inputs = centred(part_keys[0], (TOKENS, D), 1.0, 6.0, ((0, 4), (1, 4)))
    out_grads = centred(part_keys[1], (TOKENS, D), 1.0, 6.0, ((0, 4), (1, 4)))
    example_ids = jax.vmap(lambda own: jnp.searchsorted(jnp.cumsum(ragged(own, EX_DEV, TOK_DEV, MOST, 1)), jnp.arange(TOK_DEV), side="right"))(jax.random.split(part_keys[2], N_DP)).reshape((N_DP, TOK_DEV)).astype(jnp.int32)
    query_inputs = centred(part_keys[3], (QTOKENS, D), 1.0, 6.0, ((0, 4), (1, 4)))
    query_grads = centred(part_keys[4], (QTOKENS, D), 1.0, 6.0, ((0, 4), (1, 4)))
    query_ids = jax.vmap(lambda own: jnp.searchsorted(jnp.cumsum(ragged(own, QEX_DEV, QTOK_DEV, QMOST, 1)), jnp.arange(QTOK_DEV), side="right"))(jax.random.split(part_keys[5], N_DP)).reshape((N_DP, QTOK_DEV)).astype(jnp.int32)
    w_gate = centred(key_list[6], (D, FF), D ** -0.5, 0.09375, ((0, 4), (1, 4)))
    w_up = centred(key_list[7], (D, FF), D ** -0.5, 0.09375, ((0, 4), (1, 4)))
    in_project = centred(key_list[8], (R, FF), FF ** -0.5, 0.046875, ((1, 4),))
    out_project = centred(key_list[9], (R, D), D ** -0.5, 0.09375, ((1, 4),))
    return dict(inputs=inputs, out_grads=out_grads, example_ids=example_ids, query_inputs=query_inputs, query_grads=query_grads, query_ids=query_ids, w_gate=w_gate, w_up=w_up, in_project=in_project, out_project=out_project)


def outer_sum(left, right, ids, count):
    onehot = (ids[:, None] == jnp.arange(count, dtype=jnp.int32)[None, :]).astype(jnp.float32)
    spread = (onehot[:, :, None] * left[:, None, :]).reshape(left.shape[0], count * left.shape[1])
    return jnp.dot(spread.T, right, precision=lax.Precision.HIGHEST).reshape(count, left.shape[1] * right.shape[1])

def sketch_block(tokens, grads, ids, count, w_gate, w_up, in_project, out_project):
    gate_act = jnp.dot(tokens, w_gate, preferred_element_type=jnp.float32)
    up_act = jnp.dot(tokens, w_up, preferred_element_type=jnp.float32)
    hidden = (jax.nn.silu(gate_act) * up_act).astype(jnp.bfloat16)
    right = jnp.dot(hidden, in_project.T, preferred_element_type=jnp.float32)
    left = jnp.dot(grads, out_project.T, preferred_element_type=jnp.float32)
    return outer_sum(left, right, ids, count)

def reference(inputs, out_grads, example_ids, query_inputs, query_grads, query_ids, w_gate, w_up, in_project, out_project):

    def train_one(items):
        return sketch_block(items[0], items[1], items[2], EX_DEV, w_gate, w_up, in_project, out_project)

    def query_one(items):
        return sketch_block(items[0], items[1], items[2], QEX_DEV, w_gate, w_up, in_project, out_project)
    sketches = lax.map(train_one, (inputs.reshape(N_DP, TOK_DEV, D), out_grads.reshape(N_DP, TOK_DEV, D), example_ids))
    sketches = sketches.reshape(EXAMPLES, R * R)
    query_sketches = lax.map(query_one, (query_inputs.reshape(N_DP, QTOK_DEV, D), query_grads.reshape(N_DP, QTOK_DEV, D), query_ids))
    query_sketches = query_sketches.reshape(QUERIES, R * R)
    train_norm = jnp.sqrt(lax.optimization_barrier(jnp.sum(sketches * sketches, axis=1)) + 1e-06)
    query_norm = jnp.sqrt(lax.optimization_barrier(jnp.sum(query_sketches * query_sketches, axis=1)) + 1e-06)
    inner = jnp.dot(sketches, query_sketches.T, precision=lax.Precision.HIGHEST)
    scores = R * inner / (train_norm[:, None] * query_norm[None, :])
    return (sketches, scores)
```

```python
import functools

import jax
import jax.numpy as jnp
from jax import lax
from jax.experimental import pallas as pl
from jax.experimental.pallas import tpu as pltpu
from jax.sharding import PartitionSpec as P

EX_DEV = 16
QEX_DEV = 16


def sketch_from(left, right, onehot):
    count = onehot.shape[1]
    spread = (onehot[:, :, None] * left[:, None, :]).reshape(left.shape[0], count * left.shape[1])
    return jnp.dot(spread.T, right, precision=lax.Precision.HIGHEST).reshape(
        count, left.shape[1] * right.shape[1]
    )


def member_table(ids, count):
    return (ids[:, None] == jnp.arange(count, dtype=jnp.int32)[None, :]).astype(jnp.float32)


def scores_from(projected, train_rows, rank, example_ids, query_ids):
    sketches = sketch_from(
        projected[:train_rows, :rank],
        projected[:train_rows, rank:],
        member_table(example_ids[0], EX_DEV),
    )
    query_part = projected[train_rows:]
    query_table = member_table(query_ids[0], QEX_DEV)
    local_sketch = sketch_from(query_part[:, :rank], query_part[:, rank:], query_table)
    query_sketches = lax.all_gather(local_sketch, "dp", axis=0, tiled=True)
    train_norm = jnp.sqrt(jnp.sum(sketches * sketches, axis=1) + 1e-06)
    query_norm = jnp.sqrt(jnp.sum(query_sketches * query_sketches, axis=1) + 1e-06)
    inner = jnp.dot(sketches, query_sketches.T, precision=lax.Precision.HIGHEST)
    scores = rank * inner / (train_norm[:, None] * query_norm[None, :])
    return (sketches, scores)


def generic_local(
    inputs,
    out_grads,
    example_ids,
    query_inputs,
    query_grads,
    query_ids,
    w_gate,
    w_up,
    in_project,
    out_project,
):
    full_train, full_query = (
        lax.all_gather(inputs, "tensor", axis=1, tiled=True),
        lax.all_gather(query_inputs, "tensor", axis=1, tiled=True),
    )
    all_tokens = jnp.concatenate([full_train, full_query], 0)
    gate_act = jnp.dot(
        all_tokens,
        lax.all_gather(w_gate, "dp", axis=0, tiled=True),
        preferred_element_type=jnp.float32,
    )
    up_act = jnp.dot(
        all_tokens,
        lax.all_gather(w_up, "dp", axis=0, tiled=True),
        preferred_element_type=jnp.float32,
    )
    hidden = (jax.nn.silu(gate_act) * up_act).astype(jnp.bfloat16)
    all_grads = jnp.concatenate([out_grads, query_grads], 0)
    partial_sum = jnp.concatenate(
        [
            jnp.dot(all_grads, out_project.T, preferred_element_type=jnp.float32),
            jnp.dot(hidden, in_project.T, preferred_element_type=jnp.float32),
        ],
        1,
    )
    projected = lax.psum(partial_sum, "tensor")
    return scores_from(projected, inputs.shape[0], in_project.shape[0], example_ids, query_ids)


CHUNK = 256
MESH = pl.DeviceIdType.MESH


def hidden_kernel(
    n_tensor, chunks, x_ref, qx_ref, wg_ref, wu_ref, proj_ref, out_ref,
    tok, wts, lx, lw, zs, zr, ys, yr, xs, xr, ss, sr, fs, fr,
):
    group = lax.axis_index("groups")
    dp = lax.axis_index("dp")
    me = lax.axis_index("tensor")
    train, cols = x_ref.shape
    rows = wg_ref.shape[0]
    base = group * (chunks * CHUNK)
    sibling = dp + 1 - 2 * (dp % 2)
    across = (dp + 2) % 4
    far = (sibling + 2) % 4

    def tok_at(slot, shard):
        return tok.at[slot, :, pl.ds(pl.multiple_of(shard * cols, cols), cols)]

    def wts_at(i, quarter):
        return wts.at[i, pl.ds(pl.multiple_of(quarter * rows, rows), rows), :]

    def z_copy(shard, way, to):
        return pltpu.make_async_remote_copy(
            tok_at(0, shard), tok_at(0, shard), zs.at[way, shard], zr.at[shard],
            device_id={"tensor": to}, device_id_type=MESH)

    def y_copy(shard):
        return pltpu.make_async_remote_copy(
            tok_at(0, shard), tok_at(1, shard), ys.at[shard], yr.at[shard],
            device_id={"groups": 1 - group}, device_id_type=MESH)

    def w_copy(i, quarter, send, recv, to):
        return pltpu.make_async_remote_copy(
            wts_at(i, quarter), wts_at(i, quarter), send.at[i], recv.at[i],
            device_id={"dp": to}, device_id_type=MESH)

    def local_w(i):
        columns = pl.ds(pl.multiple_of(base + i * CHUNK, CHUNK // 2), CHUNK)
        mine = pl.ds(pl.multiple_of(dp * rows, rows), rows)
        return (
            pltpu.make_async_copy(wg_ref.at[:, columns], wts.at[i, mine, pl.ds(0, CHUNK)], lw.at[0, i]),
            pltpu.make_async_copy(wu_ref.at[:, columns], wts.at[i, mine, pl.ds(CHUNK, CHUNK)], lw.at[1, i]),
        )

    own = pl.ds(pl.multiple_of(me * cols, cols), cols)
    local_x = (
        pltpu.make_async_copy(x_ref, tok.at[0, pl.ds(0, train), own], lx.at[0]),
        pltpu.make_async_copy(qx_ref, tok.at[0, pl.ds(train, qx_ref.shape[0]), own], lx.at[1]),
    )
    for copy in local_x:
        copy.start()

    @pl.loop(0, chunks)
    def _(i):
        for copy in local_w(i):
            copy.start()

    barrier = pltpu.get_barrier_semaphore()
    for target in ({"dp": sibling}, {"dp": across}, {"groups": 1 - group}):
        pl.semaphore_signal(barrier, inc=1, device_id=target, device_id_type=MESH)

    @pl.when(me > 0)
    def _():
        pl.semaphore_signal(barrier, inc=1, device_id={"tensor": me - 1}, device_id_type=MESH)

    @pl.when(me < n_tensor - 1)
    def _():
        pl.semaphore_signal(barrier, inc=1, device_id={"tensor": me + 1}, device_id_type=MESH)

    pl.semaphore_wait(barrier, 3 + (me + n_tensor - 1) // n_tensor + (2 * n_tensor - 2 - me) // n_tensor)

    for copy in local_x:
        copy.wait()

    def pass_right(shard):
        @pl.when(me < n_tensor - 1)
        def _():
            z_copy(shard, 0, me + 1).start()

    def pass_left(shard):
        @pl.when(me > 0)
        def _():
            z_copy(shard, 1, me - 1).start()

    pass_right(me)
    pass_left(me)
    y_copy(me).start()

    @pl.loop(0, chunks)
    def _(i):
        for copy in local_w(i):
            copy.wait()
        w_copy(i, dp, xs, xr, across).start()
        w_copy(i, dp, ss, sr, sibling).start()

    out_ref[...] = jnp.zeros_like(out_ref)

    def hop(h):
        @pl.when(me >= h)
        def _():
            z_copy(me - h, 0, me).wait_recv()
            pass_right(me - h)
            y_copy(me - h).start()

        @pl.when(me + h < n_tensor)
        def _():
            z_copy(me + h, 1, me).wait_recv()
            pass_left(me + h)
            y_copy(me + h).start()

    def hand_on(i):
        w_copy(i, across, xs, xr, across).wait_recv()
        w_copy(i, across, fs, fr, sibling).start()

    def arrive(i):
        w_copy(i, sibling, ss, sr, sibling).wait_recv()
        w_copy(i, far, fs, fr, sibling).wait_recv()

    def work(slot, i):
        both = jnp.dot(tok[slot], wts[i], preferred_element_type=jnp.float32)
        gate, up = both[:, :CHUNK], both[:, CHUNK:]
        hidden = (gate / (1.0 + jnp.exp(-gate)) * up).astype(jnp.bfloat16)
        part = proj_ref[:, pl.ds(pl.multiple_of(base + i * CHUNK, CHUNK // 2), CHUNK)]
        out_ref[slot] += lax.dot_general(
            hidden, part, (((1,), (1,)), ((), ())), preferred_element_type=jnp.float32)

    early = chunks // 2 + 1
    done = 0
    for h in range(1, n_tensor):
        upto = max(done, min(early, (early * h) // (n_tensor - 1)))
        for i in range(done, upto):
            hand_on(i)
        done = upto
        hop(h)

    @pl.loop(0, chunks - 1)
    def _(i):
        @pl.when(i >= early)
        def _():
            hand_on(i)

        arrive(i)
        work(0, i)

    @pl.loop(0, n_tensor)
    def _(shard):
        y_copy(shard).wait_recv()

    @pl.loop(0, chunks + 1)
    def _(i):
        @pl.when(i == chunks - 1)
        def _():
            hand_on(chunks - 1)
            arrive(chunks - 1)

        work(1 - i // chunks, i - i // chunks)

    @pl.loop(0, chunks)
    def _(i):
        w_copy(i, dp, xs, xr, across).wait_send()
        w_copy(i, dp, ss, sr, sibling).wait_send()
        w_copy(i, across, fs, fr, sibling).wait_send()

    for shard in range(n_tensor):
        y_copy(shard).wait_send()

        @pl.when((shard <= me) & (me < n_tensor - 1))
        def _():
            z_copy(shard, 0, me).wait_send()

        @pl.when((shard >= me) & (me > 0))
        def _():
            z_copy(shard, 1, me).wait_send()


def hidden_products(n_tensor, inputs, query_inputs, w_gate, w_up, in_project):
    tokens = inputs.shape[0] + query_inputs.shape[0]
    rank = in_project.shape[0]
    rows, units = w_gate.shape
    chunks = units // 2 // CHUNK
    anywhere = pl.BlockSpec(memory_space=pl.ANY)
    vmem = pl.BlockSpec(memory_space=pltpu.VMEM)
    dma = pltpu.SemaphoreType.DMA
    return pl.pallas_call(
        functools.partial(hidden_kernel, n_tensor, chunks),
        out_shape=jax.ShapeDtypeStruct((2, tokens, rank), jnp.float32),
        in_specs=[anywhere] * 4 + [vmem],
        out_specs=vmem,
        scratch_shapes=[
            pltpu.VMEM((2, tokens, inputs.shape[1] * n_tensor), jnp.bfloat16),
            pltpu.VMEM((chunks, rows * 4, 2 * CHUNK), jnp.bfloat16),
            dma((2,)), dma((2, chunks)), dma((2, n_tensor)), dma((n_tensor,)),
            dma((n_tensor,)), dma((n_tensor,)),
        ] + [dma((chunks,))] * 6,
        compiler_params=pltpu.CompilerParams(
            collective_id=0, has_side_effects=True, vmem_limit_bytes=60 * 2**20),
        name="hidden_products",
    )(inputs, query_inputs, w_gate, w_up, in_project)


def fused_local(
    n_tensor,
    inputs,
    out_grads,
    example_ids,
    query_inputs,
    query_grads,
    query_ids,
    w_gate,
    w_up,
    in_project,
    out_project,
):
    right = hidden_products(n_tensor, inputs, query_inputs, w_gate, w_up, in_project)
    all_grads = jnp.concatenate([out_grads, query_grads], 0)
    left = jnp.dot(all_grads, out_project.T, preferred_element_type=jnp.float32)
    right_own = right[0] + lax.ppermute(right[1], "groups", [(0, 1), (1, 0)])
    projected = lax.psum(jnp.concatenate([left, right_own], 1), "tensor")
    return scores_from(projected, inputs.shape[0], in_project.shape[0], example_ids, query_ids)


def solution(mesh):
    n_tensor = mesh.shape["tensor"]
    paired = mesh.shape["groups"] == 2 and mesh.shape["dp"] == 4

    def local(*args):
        w_gate = args[6]
        if paired and w_gate.shape[1] % (2 * CHUNK) == 0:
            return fused_local(n_tensor, *args)
        return generic_local(*args)

    in_specs = (
        P(("groups", "dp"), "tensor"),
        P(("groups", "dp"), "tensor"),
        P(("groups", "dp"), None),
        P(("groups", "dp"), "tensor"),
        P(("groups", "dp"), "tensor"),
        P(("groups", "dp"), None),
        P("dp", "tensor"),
        P("dp", "tensor"),
        P(None, "tensor"),
        P(None, "tensor"),
    )
    out_specs = (P(("groups", "dp"), None), P(("groups", "dp"), None))
    return jax.shard_map(local, mesh=mesh, in_specs=in_specs, out_specs=out_specs, check_vma=False)
```

```python
import functools

import jax
import jax.numpy as jnp
from jax import lax
from jax.experimental import pallas as pl
from jax.experimental.pallas import tpu as pltpu
from jax.sharding import PartitionSpec as P

EX_DEV = 16
QEX_DEV = 16


def sketch_from(left, right, onehot):
    count = onehot.shape[1]
    spread = (onehot[:, :, None] * left[:, None, :]).reshape(left.shape[0], count * left.shape[1])
    return jnp.dot(spread.T, right, precision=lax.Precision.HIGHEST).reshape(
        count, left.shape[1] * right.shape[1]
    )


def member_table(ids, count):
    return (ids[:, None] == jnp.arange(count, dtype=jnp.int32)[None, :]).astype(jnp.float32)


def scores_from(projected, train_rows, rank, example_ids, query_ids):
    sketches = sketch_from(
        projected[:train_rows, :rank],
        projected[:train_rows, rank:],
        member_table(example_ids[0], EX_DEV),
    )
    query_part = projected[train_rows:]
    query_table = member_table(query_ids[0], QEX_DEV)
    local_sketch = sketch_from(query_part[:, :rank], query_part[:, rank:], query_table)
    query_sketches = lax.all_gather(local_sketch, "dp", axis=0, tiled=True)
    return sketches, scores_of(sketches, query_sketches, rank)


def scores_of(sketches, query_sketches, rank):
    train_norm = jnp.sqrt(jnp.sum(sketches * sketches, axis=1) + 1e-06)
    query_norm = jnp.sqrt(jnp.sum(query_sketches * query_sketches, axis=1) + 1e-06)
    inner = jnp.dot(sketches, query_sketches.T, precision=lax.Precision.HIGHEST)
    scores = rank * inner / (train_norm[:, None] * query_norm[None, :])
    return scores


def generic_local(
    inputs,
    out_grads,
    example_ids,
    query_inputs,
    query_grads,
    query_ids,
    w_gate,
    w_up,
    in_project,
    out_project,
):
    full_train, full_query = (
        lax.all_gather(inputs, "tensor", axis=1, tiled=True),
        lax.all_gather(query_inputs, "tensor", axis=1, tiled=True),
    )
    all_tokens = jnp.concatenate([full_train, full_query], 0)
    gate_act = jnp.dot(
        all_tokens,
        lax.all_gather(w_gate, "dp", axis=0, tiled=True),
        preferred_element_type=jnp.float32,
    )
    up_act = jnp.dot(
        all_tokens,
        lax.all_gather(w_up, "dp", axis=0, tiled=True),
        preferred_element_type=jnp.float32,
    )
    hidden = (jax.nn.silu(gate_act) * up_act).astype(jnp.bfloat16)
    all_grads = jnp.concatenate([out_grads, query_grads], 0)
    partial_sum = jnp.concatenate(
        [
            jnp.dot(all_grads, out_project.T, preferred_element_type=jnp.float32),
            jnp.dot(hidden, in_project.T, preferred_element_type=jnp.float32),
        ],
        1,
    )
    projected = lax.psum(partial_sum, "tensor")
    return scores_from(projected, inputs.shape[0], in_project.shape[0], example_ids, query_ids)


CHUNK = 256
MESH = pl.DeviceIdType.MESH


def sketch_kernel(
    n_tensor, chunks, x_ref, qx_ref, wg_ref, wu_ref, dy_ref, qdy_ref, proj_ref, oproj_ref, ids_ref, qids_ref,
    sketch_ref, queries_ref,
    tok, wts, grads, acc, lefts, swap, parts, terms, whole,
    lx, lw, zs, zr, ys, yr, xs, xr, ss, sr, fs, fr, lg, ls, lr, ps, pr, ts, tr, ws, wr, qs, qr,
):
    group = lax.axis_index("groups")
    dp = lax.axis_index("dp")
    me = lax.axis_index("tensor")
    train, cols = x_ref.shape
    rows = wg_ref.shape[0]
    base = group * (chunks * CHUNK)
    sibling = dp + 1 - 2 * (dp % 2)
    across = (dp + 2) % 4
    far = (sibling + 2) % 4

    def tok_at(slot, shard):
        return tok.at[slot, :, pl.ds(pl.multiple_of(shard * cols, cols), cols)]

    def wts_at(i, quarter):
        return wts.at[i, pl.ds(pl.multiple_of(quarter * rows, rows), rows), :]

    def z_copy(shard, way, to):
        return pltpu.make_async_remote_copy(
            tok_at(0, shard), tok_at(0, shard), zs.at[way, shard], zr.at[shard],
            device_id={"tensor": to}, device_id_type=MESH)

    def y_copy(shard):
        return pltpu.make_async_remote_copy(
            tok_at(0, shard), tok_at(1, shard), ys.at[shard], yr.at[shard],
            device_id={"groups": 1 - group}, device_id_type=MESH)

    def w_copy(i, quarter, send, recv, to):
        return pltpu.make_async_remote_copy(
            wts_at(i, quarter), wts_at(i, quarter), send.at[i], recv.at[i],
            device_id={"dp": to}, device_id_type=MESH)

    def local_w(i):
        columns = pl.ds(pl.multiple_of(base + i * CHUNK, CHUNK // 2), CHUNK)
        mine = pl.ds(pl.multiple_of(dp * rows, rows), rows)
        return (
            pltpu.make_async_copy(wg_ref.at[:, columns], wts.at[i, mine, pl.ds(0, CHUNK)], lw.at[0, i]),
            pltpu.make_async_copy(wu_ref.at[:, columns], wts.at[i, mine, pl.ds(CHUNK, CHUNK)], lw.at[1, i]),
        )

    own = pl.ds(pl.multiple_of(me * cols, cols), cols)
    local_x = (
        pltpu.make_async_copy(x_ref, tok.at[0, pl.ds(0, train), own], lx.at[0]),
        pltpu.make_async_copy(qx_ref, tok.at[0, pl.ds(train, qx_ref.shape[0]), own], lx.at[1]),
    )
    local_g = (
        pltpu.make_async_copy(dy_ref, grads.at[pl.ds(0, train)], lg.at[0]),
        pltpu.make_async_copy(qdy_ref, grads.at[pl.ds(train, qdy_ref.shape[0])], lg.at[1]),
    )
    for copy in local_x:
        copy.start()

    @pl.loop(0, chunks)
    def _(i):
        for copy in local_w(i):
            copy.start()

    barrier = pltpu.get_barrier_semaphore()
    targets = [{"groups": 1 - group}]
    targets += [{"dp": (dp + step) % 4} for step in range(1, 4)]
    targets += [{"tensor": (me + step) % n_tensor} for step in range(1, n_tensor)]
    for target in targets:
        pl.semaphore_signal(barrier, inc=1, device_id=target, device_id_type=MESH)
    for copy in local_g:
        copy.start()
    pl.semaphore_wait(barrier, len(targets))

    for copy in local_x:
        copy.wait()

    def pass_right(shard):
        @pl.when(me < n_tensor - 1)
        def _():
            z_copy(shard, 0, me + 1).start()

    def pass_left(shard):
        @pl.when(me > 0)
        def _():
            z_copy(shard, 1, me - 1).start()

    pass_right(me)
    pass_left(me)
    y_copy(me).start()

    @pl.loop(0, chunks)
    def _(i):
        for copy in local_w(i):
            copy.wait()
        w_copy(i, dp, xs, xr, across).start()
        w_copy(i, dp, ss, sr, sibling).start()

    acc[...] = jnp.zeros_like(acc)
    for copy in local_g:
        copy.wait()
    lefts[me] = lax.dot_general(
        oproj_ref[...], grads[...], (((1,), (1,)), ((), ())), preferred_element_type=jnp.float32)

    def hop(h):
        @pl.when(me >= h)
        def _():
            z_copy(me - h, 0, me).wait_recv()
            pass_right(me - h)
            y_copy(me - h).start()

        @pl.when(me + h < n_tensor)
        def _():
            z_copy(me + h, 1, me).wait_recv()
            pass_left(me + h)
            y_copy(me + h).start()

    def hand_on(i):
        w_copy(i, across, xs, xr, across).wait_recv()
        w_copy(i, across, fs, fr, sibling).start()

    def arrive(i):
        w_copy(i, sibling, ss, sr, sibling).wait_recv()
        w_copy(i, far, fs, fr, sibling).wait_recv()

    def work(slot, i):
        both = jnp.dot(tok[slot], wts[i], preferred_element_type=jnp.float32)
        gate, up = both[:, :CHUNK], both[:, CHUNK:]
        hidden = (gate / (1.0 + jnp.exp(-gate)) * up).astype(jnp.bfloat16)
        part = proj_ref[:, pl.ds(pl.multiple_of(base + i * CHUNK, CHUNK // 2), CHUNK)]
        acc[slot] += lax.dot_general(
            hidden, part, (((1,), (1,)), ((), ())), preferred_element_type=jnp.float32)

    early = chunks // 2 + 1
    done = 0
    for h in range(1, n_tensor):
        upto = max(done, min(early, (early * h) // (n_tensor - 1)))
        for i in range(done, upto):
            hand_on(i)
        done = upto
        hop(h)

    def others():
        return [(me + step) % n_tensor for step in range(1, n_tensor)]

    def left_copy(source, to):
        return pltpu.make_async_remote_copy(
            lefts.at[source], lefts.at[source], ls.at[to], lr.at[source],
            device_id={"tensor": to}, device_id_type=MESH)

    def swap_copy():
        return pltpu.make_async_remote_copy(
            swap.at[0], swap.at[1], ps.at[0], pr.at[0], device_id={"groups": 1 - group}, device_id_type=MESH)

    def term_copy(source, to):
        return pltpu.make_async_remote_copy(
            parts.at[to], terms.at[source], ts.at[to], tr.at[source],
            device_id={"tensor": to}, device_id_type=MESH)

    def whole_copy(source, to):
        return pltpu.make_async_remote_copy(
            whole.at[source], whole.at[source], ws.at[to], wr.at[source],
            device_id={"tensor": to}, device_id_type=MESH)

    def query_copy(source, to):
        return pltpu.make_async_remote_copy(
            queries_ref.at[source], queries_ref.at[source], qs.at[to], qr.at[source],
            device_id={"dp": to}, device_id_type=MESH)

    for to in others():
        left_copy(me, to).start()

    @pl.loop(0, chunks - 1)
    def _(i):
        @pl.when(i >= early)
        def _():
            hand_on(i)

        arrive(i)
        work(0, i)

    @pl.loop(0, n_tensor)
    def _(shard):
        y_copy(shard).wait_recv()

    @pl.loop(0, chunks - 1)
    def _(i):
        work(1, i)

    hand_on(chunks - 1)
    arrive(chunks - 1)
    half = tok.shape[1] // 2
    rank = proj_ref.shape[0]

    def packed(slot):
        return jnp.concatenate([acc[slot, :half], acc[slot, half:]], axis=1)

    @pl.loop(0, 2)
    def _(turn):
        work(1 - turn, chunks - 1)

        @pl.when(turn == 0)
        def _():
            swap[0] = packed(1)
            swap_copy().start()

    swap_copy().wait_recv()
    parts[...] = (packed(0) + swap[1]).reshape(parts.shape)
    for to in others():
        term_copy(me, to).start()
    total = parts[me]
    for source in others():
        term_copy(source, source).wait_recv()
        total = total + terms[source]
    whole[me] = total
    for to in others():
        whole_copy(me, to).start()
    for source in others():
        left_copy(source, source).wait_recv()
    left = lefts[0]
    for source in range(1, n_tensor):
        left = left + lefts[source]
    for source in others():
        whole_copy(source, source).wait_recv()
    both = whole[...].reshape(half, 2 * rank)
    right = jnp.concatenate([both[:, :rank], both[:, rank:]], axis=0)

    def outer_sums(left, right, ids, count):
        sums = []
        for side in range(2):
            some = left[side * (rank // 2):(side + 1) * (rank // 2)]
            spread = jnp.concatenate([jnp.where(ids == e, some, 0.0) for e in range(count)], axis=0)
            sums.append(jnp.dot(
                spread, right, precision=lax.Precision.HIGHEST, preferred_element_type=jnp.float32))
        return jnp.concatenate(sums, axis=1)

    queries_ref[dp] = outer_sums(left[:, train:], right[train:], qids_ref[...], QEX_DEV)
    for step in range(1, 4):
        query_copy(dp, (dp + step) % 4).start()
    sketch_ref[...] = outer_sums(left[:, :train], right[:train], ids_ref[...], EX_DEV)
    for step in range(1, 4):
        query_copy((dp + step) % 4, (dp + step) % 4).wait_recv()

    for to in others():
        left_copy(me, to).wait_send()
        term_copy(me, to).wait_send()
        whole_copy(me, to).wait_send()
    swap_copy().wait_send()
    for step in range(1, 4):
        query_copy(dp, (dp + step) % 4).wait_send()

    @pl.loop(0, chunks)
    def _(i):
        w_copy(i, dp, xs, xr, across).wait_send()
        w_copy(i, dp, ss, sr, sibling).wait_send()
        w_copy(i, across, fs, fr, sibling).wait_send()

    for shard in range(n_tensor):
        y_copy(shard).wait_send()

        @pl.when((shard <= me) & (me < n_tensor - 1))
        def _():
            z_copy(shard, 0, me).wait_send()

        @pl.when((shard >= me) & (me > 0))
        def _():
            z_copy(shard, 1, me).wait_send()


def sketch_products(
    n_tensor, inputs, out_grads, example_ids, query_inputs, query_grads, query_ids, w_gate, w_up, in_project, out_project
):
    tokens = inputs.shape[0] + query_inputs.shape[0]
    rank = in_project.shape[0]
    rows, units = w_gate.shape
    chunks = units // 2 // CHUNK
    anywhere = pl.BlockSpec(memory_space=pl.ANY)
    vmem = pl.BlockSpec(memory_space=pltpu.VMEM)
    dma = pltpu.SemaphoreType.DMA
    f32 = jnp.float32
    return pl.pallas_call(
        functools.partial(sketch_kernel, n_tensor, chunks),
        out_shape=(
            jax.ShapeDtypeStruct((EX_DEV * rank // 2, 2 * rank), f32),
            jax.ShapeDtypeStruct((4, QEX_DEV * rank // 2, 2 * rank), f32),
        ),
        in_specs=[anywhere] * 6 + [vmem] * 4,
        out_specs=(vmem, vmem),
        scratch_shapes=[
            pltpu.VMEM((2, tokens, inputs.shape[1] * n_tensor), jnp.bfloat16),
            pltpu.VMEM((chunks, rows * 4, 2 * CHUNK), jnp.bfloat16),
            pltpu.VMEM((tokens, out_grads.shape[1]), jnp.bfloat16),
            pltpu.VMEM((2, tokens, rank), f32),
            pltpu.VMEM((n_tensor, rank, tokens), f32),
            pltpu.VMEM((2, tokens // 2, 2 * rank), f32),
            pltpu.VMEM((n_tensor, tokens // 2 // n_tensor, 2 * rank), f32),
            pltpu.VMEM((n_tensor, tokens // 2 // n_tensor, 2 * rank), f32),
            pltpu.VMEM((n_tensor, tokens // 2 // n_tensor, 2 * rank), f32),
            dma((2,)), dma((2, chunks)), dma((2, n_tensor)), dma((n_tensor,)),
            dma((n_tensor,)), dma((n_tensor,)),
        ] + [dma((chunks,))] * 6 + [dma((2,))] + [dma((n_tensor,))] * 2 + [dma((1,))] * 2
        + [dma((n_tensor,))] * 4 + [dma((4,))] * 2,
        compiler_params=pltpu.CompilerParams(
            collective_id=0, has_side_effects=True, vmem_limit_bytes=60 * 2**20),
        name="sketch_products",
    )(inputs, query_inputs, w_gate, w_up, out_grads, query_grads, in_project, out_project, example_ids, query_ids)


def fused_local(n_tensor, *args):
    train, queries = sketch_products(n_tensor, *args)
    rank = args[8].shape[0]

    def unpacked(pairs):
        return pairs.reshape(-1, rank // 2, 2, rank).transpose(0, 2, 1, 3).reshape(-1, rank * rank)

    sketches = unpacked(train)
    return sketches, scores_of(sketches, unpacked(queries), rank)


def solution(mesh):
    n_tensor = mesh.shape["tensor"]
    paired = mesh.shape["groups"] == 2 and mesh.shape["dp"] == 4

    def local(*args):
        w_gate = args[6]
        if paired and w_gate.shape[1] % (2 * CHUNK) == 0:
            return fused_local(n_tensor, *args)
        return generic_local(*args)

    in_specs = (
        P(("groups", "dp"), "tensor"),
        P(("groups", "dp"), "tensor"),
        P(("groups", "dp"), None),
        P(("groups", "dp"), "tensor"),
        P(("groups", "dp"), "tensor"),
        P(("groups", "dp"), None),
        P("dp", "tensor"),
        P("dp", "tensor"),
        P(None, "tensor"),
        P(None, "tensor"),
    )
    out_specs = (P(("groups", "dp"), None), P(("groups", "dp"), None))
    return jax.shard_map(local, mesh=mesh, in_specs=in_specs, out_specs=out_specs, check_vma=False)
```

```python
import functools

import jax
import jax.numpy as jnp
from jax import lax
from jax.experimental import pallas as pl
from jax.experimental.pallas import tpu as pltpu
from jax.sharding import PartitionSpec as P

EX_DEV = 16
QEX_DEV = 16


def sketch_from(left, right, onehot):
    count = onehot.shape[1]
    spread = (onehot[:, :, None] * left[:, None, :]).reshape(left.shape[0], count * left.shape[1])
    return jnp.dot(spread.T, right, precision=lax.Precision.HIGHEST).reshape(
        count, left.shape[1] * right.shape[1]
    )


def member_table(ids, count):
    return (ids[:, None] == jnp.arange(count, dtype=jnp.int32)[None, :]).astype(jnp.float32)


def scores_from(projected, train_rows, rank, example_ids, query_ids):
    sketches = sketch_from(
        projected[:train_rows, :rank],
        projected[:train_rows, rank:],
        member_table(example_ids[0], EX_DEV),
    )
    query_part = projected[train_rows:]
    query_table = member_table(query_ids[0], QEX_DEV)
    local_sketch = sketch_from(query_part[:, :rank], query_part[:, rank:], query_table)
    query_sketches = lax.all_gather(local_sketch, "dp", axis=0, tiled=True)
    return sketches, scores_of(sketches, query_sketches, rank)


def scores_of(sketches, query_sketches, rank):
    train_norm = jnp.sqrt(jnp.sum(sketches * sketches, axis=1) + 1e-06)
    query_norm = jnp.sqrt(jnp.sum(query_sketches * query_sketches, axis=1) + 1e-06)
    inner = jnp.dot(sketches, query_sketches.T, precision=lax.Precision.HIGHEST)
    scores = rank * inner / (train_norm[:, None] * query_norm[None, :])
    return scores


def generic_local(
    inputs,
    out_grads,
    example_ids,
    query_inputs,
    query_grads,
    query_ids,
    w_gate,
    w_up,
    in_project,
    out_project,
):
    full_train, full_query = (
        lax.all_gather(inputs, "tensor", axis=1, tiled=True),
        lax.all_gather(query_inputs, "tensor", axis=1, tiled=True),
    )
    all_tokens = jnp.concatenate([full_train, full_query], 0)
    gate_act = jnp.dot(
        all_tokens,
        lax.all_gather(w_gate, "dp", axis=0, tiled=True),
        preferred_element_type=jnp.float32,
    )
    up_act = jnp.dot(
        all_tokens,
        lax.all_gather(w_up, "dp", axis=0, tiled=True),
        preferred_element_type=jnp.float32,
    )
    hidden = (jax.nn.silu(gate_act) * up_act).astype(jnp.bfloat16)
    all_grads = jnp.concatenate([out_grads, query_grads], 0)
    partial_sum = jnp.concatenate(
        [
            jnp.dot(all_grads, out_project.T, preferred_element_type=jnp.float32),
            jnp.dot(hidden, in_project.T, preferred_element_type=jnp.float32),
        ],
        1,
    )
    projected = lax.psum(partial_sum, "tensor")
    return scores_from(projected, inputs.shape[0], in_project.shape[0], example_ids, query_ids)


CHUNK = 256
MESH = pl.DeviceIdType.MESH


def sketch_kernel(
    n_tensor, chunks, x_ref, qx_ref, wg_ref, wu_ref, dy_ref, qdy_ref, proj_ref, oproj_ref, ids_ref, qids_ref,
    sketch_ref, scores_ref,
    tok, wts, grads, acc, lefts, swap, parts, terms, whole,
    halfway, spreads, grams, lqs, rqs, norms, idrows,
    lx, lw, zs, zr, ys, yr, xs, xr, ss, sr, fs, fr, lg, ls, lr, ps, pr, ts, tr, ws, wr, qs, qr, ns, nr, ds, dr, es, er,
):
    group = lax.axis_index("groups")
    dp = lax.axis_index("dp")
    me = lax.axis_index("tensor")
    train, cols = x_ref.shape
    rows = wg_ref.shape[0]
    base = group * (chunks * CHUNK)
    sibling = dp + 1 - 2 * (dp % 2)
    across = (dp + 2) % 4
    far = (sibling + 2) % 4

    def tok_at(slot, shard):
        return tok.at[slot, :, pl.ds(pl.multiple_of(shard * cols, cols), cols)]

    def wts_at(i, quarter):
        return wts.at[i, pl.ds(pl.multiple_of(quarter * rows, rows), rows), :]

    def z_copy(shard, way, to):
        return pltpu.make_async_remote_copy(
            tok_at(0, shard), tok_at(0, shard), zs.at[way, shard], zr.at[shard],
            device_id={"tensor": to}, device_id_type=MESH)

    def y_copy(shard):
        return pltpu.make_async_remote_copy(
            tok_at(0, shard), tok_at(1, shard), ys.at[shard], yr.at[shard],
            device_id={"groups": 1 - group}, device_id_type=MESH)

    def w_copy(i, quarter, send, recv, to):
        return pltpu.make_async_remote_copy(
            wts_at(i, quarter), wts_at(i, quarter), send.at[i], recv.at[i],
            device_id={"dp": to}, device_id_type=MESH)

    def local_w(i):
        columns = pl.ds(pl.multiple_of(base + i * CHUNK, CHUNK // 2), CHUNK)
        mine = pl.ds(pl.multiple_of(dp * rows, rows), rows)
        return (
            pltpu.make_async_copy(wg_ref.at[:, columns], wts.at[i, mine, pl.ds(0, CHUNK)], lw.at[0, i]),
            pltpu.make_async_copy(wu_ref.at[:, columns], wts.at[i, mine, pl.ds(CHUNK, CHUNK)], lw.at[1, i]),
        )

    own = pl.ds(pl.multiple_of(me * cols, cols), cols)
    local_x = (
        pltpu.make_async_copy(x_ref, tok.at[0, pl.ds(0, train), own], lx.at[0]),
        pltpu.make_async_copy(qx_ref, tok.at[0, pl.ds(train, qx_ref.shape[0]), own], lx.at[1]),
    )
    local_g = (
        pltpu.make_async_copy(dy_ref, grads.at[pl.ds(0, train)], lg.at[0]),
        pltpu.make_async_copy(qdy_ref, grads.at[pl.ds(train, qdy_ref.shape[0])], lg.at[1]),
    )
    for copy in local_x:
        copy.start()

    @pl.loop(0, chunks)
    def _(i):
        for copy in local_w(i):
            copy.start()

    barrier = pltpu.get_barrier_semaphore()
    targets = [{"groups": 1 - group}]
    targets += [{"dp": (dp + step) % 4} for step in range(1, 4)]
    targets += [{"tensor": (me + step) % n_tensor} for step in range(1, n_tensor)]
    for target in targets:
        pl.semaphore_signal(barrier, inc=1, device_id=target, device_id_type=MESH)
    for copy in local_g:
        copy.start()
    pl.semaphore_wait(barrier, len(targets))

    for copy in local_x:
        copy.wait()

    def pass_right(shard):
        @pl.when(me < n_tensor - 1)
        def _():
            z_copy(shard, 0, me + 1).start()

    def pass_left(shard):
        @pl.when(me > 0)
        def _():
            z_copy(shard, 1, me - 1).start()

    pass_right(me)
    pass_left(me)
    y_copy(me).start()

    @pl.loop(0, chunks)
    def _(i):
        for copy in local_w(i):
            copy.wait()
        w_copy(i, dp, xs, xr, across).start()
        w_copy(i, dp, ss, sr, sibling).start()

    acc[...] = jnp.zeros_like(acc)
    for copy in local_g:
        copy.wait()
    lefts[me] = lax.dot_general(
        oproj_ref[...], grads[...], (((1,), (1,)), ((), ())), preferred_element_type=jnp.float32)

    def hop(h):
        @pl.when(me >= h)
        def _():
            z_copy(me - h, 0, me).wait_recv()
            pass_right(me - h)
            y_copy(me - h).start()

        @pl.when(me + h < n_tensor)
        def _():
            z_copy(me + h, 1, me).wait_recv()
            pass_left(me + h)
            y_copy(me + h).start()

    def hand_on(i):
        w_copy(i, across, xs, xr, across).wait_recv()
        w_copy(i, across, fs, fr, sibling).start()

    def arrive(i):
        w_copy(i, sibling, ss, sr, sibling).wait_recv()
        w_copy(i, far, fs, fr, sibling).wait_recv()

    def finish(slot, i, both):
        gate, up = both[:, :CHUNK], both[:, CHUNK:]
        hidden = (gate / (1.0 + jnp.exp(-gate)) * up).astype(jnp.bfloat16)
        part = proj_ref[:, pl.ds(pl.multiple_of(base + i * CHUNK, CHUNK // 2), CHUNK)]
        acc[slot] += lax.dot_general(
            hidden, part, (((1,), (1,)), ((), ())), preferred_element_type=jnp.float32)

    def work(slot, i):
        finish(slot, i, jnp.dot(tok[slot], wts[i], preferred_element_type=jnp.float32))

    def side_dot(slot, i, side):
        return jnp.dot(
            tok[slot, :, pl.ds(pl.multiple_of(side * (2 * rows), 2 * rows), 2 * rows)],
            wts[i, pl.ds(pl.multiple_of(side * (2 * rows), 2 * rows), 2 * rows), :],
            preferred_element_type=jnp.float32)

    early = chunks // 2 + 1
    done = 0
    for h in range(1, n_tensor):
        upto = max(done, min(early, (early * h) // (n_tensor - 1)))
        for i in range(done, upto):
            hand_on(i)
        done = upto
        hop(h)

    def others():
        return [(me + step) % n_tensor for step in range(1, n_tensor)]

    def left_copy(source, to):
        return pltpu.make_async_remote_copy(
            lefts.at[source], lefts.at[source], ls.at[to], lr.at[source],
            device_id={"tensor": to}, device_id_type=MESH)

    def swap_copy():
        return pltpu.make_async_remote_copy(
            swap.at[0], swap.at[1], ps.at[0], pr.at[0], device_id={"groups": 1 - group}, device_id_type=MESH)

    def term_copy(source, to):
        return pltpu.make_async_remote_copy(
            parts.at[to], terms.at[source], ts.at[to], tr.at[source],
            device_id={"tensor": to}, device_id_type=MESH)

    def whole_copy(source, to):
        return pltpu.make_async_remote_copy(
            whole.at[source], whole.at[source], ws.at[to], wr.at[source],
            device_id={"tensor": to}, device_id_type=MESH)

    def dp_copy(buffer, send, recv, source, to):
        return pltpu.make_async_remote_copy(
            buffer.at[source], buffer.at[source], send.at[to], recv.at[source],
            device_id={"dp": to}, device_id_type=MESH)

    idrows[dp] = qids_ref[...]
    elsewhere = [(dp + step) % 4 for step in range(1, 4)]
    for to in elsewhere:
        dp_copy(idrows, ds, dr, dp, to).start()
    for to in others():
        left_copy(me, to).start()

    @pl.loop(0, chunks - 1)
    def _(i):
        @pl.when(i >= early)
        def _():
            hand_on(i)

        arrive(i)
        work(0, i)

    rank = proj_ref.shape[0]
    half = tok.shape[1] // 2
    for source in others():
        left_copy(source, source).wait_recv()
    left = lefts[0]
    for source in range(1, n_tensor):
        left = left + lefts[source]
    lqs[dp] = left[:, train:]
    dp_copy(lqs, es, er, dp, sibling).start()
    dp_copy(lqs, es, er, dp, across).start()

    def spread(left, ids, count, at, size):
        for side in range(2):
            some = left[side * (rank // 2):(side + 1) * (rank // 2)]
            top = some.astype(jnp.bfloat16).astype(jnp.float32)
            for k, piece in enumerate((top, some - top)):
                rows_of = [jnp.where(ids == e, piece, 0.0) for e in range(count)]
                spreads[k, side, :, pl.ds(at, size)] = jnp.concatenate(rows_of, axis=0).astype(jnp.bfloat16)

    spread(left[:, :train], ids_ref[...], EX_DEV, 0, train)
    spread(left[:, train:], qids_ref[...], QEX_DEV, train, left.shape[1] - train)
    dp_copy(lqs, es, er, across, across).wait_recv()
    far_copy = pltpu.make_async_remote_copy(
        lqs.at[across], lqs.at[across], es.at[far], er.at[across],
        device_id={"dp": sibling}, device_id_type=MESH)
    far_copy.start()
    dp_copy(lqs, es, er, sibling, sibling).wait_recv()
    dp_copy(lqs, es, er, far, far).wait_recv()
    for k in range(4):
        grams[k] = lax.dot_general(
            left[:, :train], lqs[k], (((0,), (0,)), ((), ())),
            precision=lax.Precision.HIGHEST, preferred_element_type=jnp.float32)

    @pl.loop(0, n_tensor)
    def _(shard):
        y_copy(shard).wait_recv()

    @pl.loop(0, chunks - 1)
    def _(i):
        work(1, i)

    last = chunks - 1
    w_copy(last, sibling, ss, sr, sibling).wait_recv()

    @pl.loop(0, 2)
    def _(slot):
        halfway[slot] = side_dot(slot, last, dp // 2)

    hand_on(last)
    w_copy(last, far, fs, fr, sibling).wait_recv()

    def packed(slot):
        return jnp.concatenate([acc[slot, :half], acc[slot, half:]], axis=1)

    @pl.loop(0, 2)
    def _(turn):
        finish(1 - turn, last, halfway[1 - turn] + side_dot(1 - turn, last, 1 - dp // 2))

        @pl.when(turn == 0)
        def _():
            swap[0] = packed(1)
            swap_copy().start()

    swap_copy().wait_recv()
    parts[...] = (packed(0) + swap[1]).reshape(parts.shape)
    for to in others():
        term_copy(me, to).start()
    total = parts[me]
    for source in others():
        term_copy(source, source).wait_recv()
        total = total + terms[source]
    whole[me] = total
    for to in others():
        whole_copy(me, to).start()
    for source in others():
        whole_copy(source, source).wait_recv()
    both = whole[...].reshape(half, 2 * rank)
    right = jnp.concatenate([both[:, :rank], both[:, rank:]], axis=0)

    rqs[dp] = right[train:]
    for to in elsewhere:
        dp_copy(rqs, qs, qr, dp, to).start()

    def split(value):
        top = value.astype(jnp.bfloat16)
        return top, (value - top.astype(jnp.float32)).astype(jnp.bfloat16)

    def outer_sums(right, at):
        top, rest = split(right)
        pair = jnp.concatenate([top, rest], axis=1)
        sums = []
        for side in range(2):
            span = pl.ds(at, right.shape[0])
            first = jnp.dot(spreads[0, side, :, span], pair, preferred_element_type=jnp.float32)
            second = jnp.dot(spreads[1, side, :, span], top, preferred_element_type=jnp.float32)
            sums.append(first[:, :rank] + first[:, rank:] + second)
        return jnp.concatenate(sums, axis=1)

    own_queries = outer_sums(right[train:], train)
    across_lanes = lax.dot_general(
        jnp.ones((8, 2 * rank), jnp.float32), own_queries * own_queries, (((1,), (1,)), ((), ())),
        precision=lax.Precision.HIGHEST, preferred_element_type=jnp.float32)
    entries = own_queries.shape[0]
    query_of = lax.broadcasted_iota(jnp.int32, (entries, 128), 0) // (entries // QEX_DEV)
    place = lax.broadcasted_iota(jnp.int32, (entries, 128), 1)
    norms[dp] = jnp.dot(
        across_lanes, (query_of == place).astype(jnp.float32),
        precision=lax.Precision.HIGHEST, preferred_element_type=jnp.float32)
    for to in elsewhere:
        dp_copy(norms, ns, nr, dp, to).start()

    sketch = outer_sums(right[:train], 0)
    sketch_ref[...] = sketch
    squares = jnp.sum((sketch * sketch).reshape(EX_DEV, sketch.shape[0] // EX_DEV, 2 * rank), axis=1)
    train_norm = jnp.sqrt(jnp.sum(squares, axis=1, keepdims=True) + 1e-06)

    for source in elsewhere:
        dp_copy(rqs, qs, qr, source, source).wait_recv()
        dp_copy(idrows, ds, dr, source, source).wait_recv()
        dp_copy(norms, ns, nr, source, source).wait_recv()

    def table(ids, count):
        return (lax.broadcasted_iota(jnp.int32, (count, ids.shape[1]), 0) == ids).astype(jnp.float32)

    examples = table(ids_ref[...], EX_DEV).astype(jnp.bfloat16)
    top, rest = split(right[:train])
    mine = jnp.concatenate([top, rest, top], axis=1)
    found = []
    for k in range(4):
        top, rest = split(rqs[k])
        theirs = jnp.concatenate([top, top, rest], axis=1)
        gram = grams[k] * lax.dot_general(
            mine, theirs, (((1,), (1,)), ((), ())), preferred_element_type=jnp.float32)
        top, rest = split(gram)
        by_example = jnp.dot(examples, top, preferred_element_type=jnp.float32) + jnp.dot(
            examples, rest, preferred_element_type=jnp.float32)
        inner = lax.dot_general(
            by_example, table(idrows[k], QEX_DEV), (((1,), (1,)), ((), ())),
            precision=lax.Precision.HIGHEST, preferred_element_type=jnp.float32)
        query_norm = jnp.sqrt(norms[k][:1, :QEX_DEV] + 1e-06)
        found.append(rank * inner / (train_norm * query_norm))
    scores_ref[...] = jnp.concatenate(found, axis=1)

    for to in others():
        left_copy(me, to).wait_send()
        term_copy(me, to).wait_send()
        whole_copy(me, to).wait_send()
    swap_copy().wait_send()
    for to in elsewhere:
        dp_copy(rqs, qs, qr, dp, to).wait_send()
        dp_copy(idrows, ds, dr, dp, to).wait_send()
        dp_copy(norms, ns, nr, dp, to).wait_send()
    dp_copy(lqs, es, er, dp, sibling).wait_send()
    dp_copy(lqs, es, er, dp, across).wait_send()
    far_copy.wait_send()

    @pl.loop(0, chunks)
    def _(i):
        w_copy(i, dp, xs, xr, across).wait_send()
        w_copy(i, dp, ss, sr, sibling).wait_send()
        w_copy(i, across, fs, fr, sibling).wait_send()

    for shard in range(n_tensor):
        y_copy(shard).wait_send()

        @pl.when((shard <= me) & (me < n_tensor - 1))
        def _():
            z_copy(shard, 0, me).wait_send()

        @pl.when((shard >= me) & (me > 0))
        def _():
            z_copy(shard, 1, me).wait_send()


def sketch_products(
    n_tensor, inputs, out_grads, example_ids, query_inputs, query_grads, query_ids, w_gate, w_up, in_project, out_project
):
    tokens = inputs.shape[0] + query_inputs.shape[0]
    rank = in_project.shape[0]
    rows, units = w_gate.shape
    chunks = units // 2 // CHUNK
    anywhere = pl.BlockSpec(memory_space=pl.ANY)
    vmem = pl.BlockSpec(memory_space=pltpu.VMEM)
    dma = pltpu.SemaphoreType.DMA
    f32 = jnp.float32
    return pl.pallas_call(
        functools.partial(sketch_kernel, n_tensor, chunks),
        out_shape=(
            jax.ShapeDtypeStruct((EX_DEV * rank // 2, 2 * rank), f32),
            jax.ShapeDtypeStruct((EX_DEV, 4 * QEX_DEV), f32),
        ),
        in_specs=[anywhere] * 6 + [vmem] * 4,
        out_specs=(vmem, vmem),
        scratch_shapes=[
            pltpu.VMEM((2, tokens, inputs.shape[1] * n_tensor), jnp.bfloat16),
            pltpu.VMEM((chunks, rows * 4, 2 * CHUNK), jnp.bfloat16),
            pltpu.VMEM((tokens, out_grads.shape[1]), jnp.bfloat16),
            pltpu.VMEM((2, tokens, rank), f32),
            pltpu.VMEM((n_tensor, rank, tokens), f32),
            pltpu.VMEM((2, tokens // 2, 2 * rank), f32),
            pltpu.VMEM((n_tensor, tokens // 2 // n_tensor, 2 * rank), f32),
            pltpu.VMEM((n_tensor, tokens // 2 // n_tensor, 2 * rank), f32),
            pltpu.VMEM((n_tensor, tokens // 2 // n_tensor, 2 * rank), f32),
            pltpu.VMEM((2, tokens, 2 * CHUNK), f32),
            pltpu.VMEM((2, 2, EX_DEV * rank // 2, tokens), jnp.bfloat16),
            pltpu.VMEM((4, inputs.shape[0], query_inputs.shape[0]), f32),
            pltpu.VMEM((4, rank, query_inputs.shape[0]), f32),
            pltpu.VMEM((4, query_inputs.shape[0], rank), f32),
            pltpu.VMEM((4, 8, 128), f32),
            pltpu.VMEM((4, 1, query_inputs.shape[0]), jnp.int32),
            dma((2,)), dma((2, chunks)), dma((2, n_tensor)), dma((n_tensor,)),
            dma((n_tensor,)), dma((n_tensor,)),
        ] + [dma((chunks,))] * 6 + [dma((2,))] + [dma((n_tensor,))] * 2 + [dma((1,))] * 2
        + [dma((n_tensor,))] * 4 + [dma((4,))] * 8,
        compiler_params=pltpu.CompilerParams(
            collective_id=0, has_side_effects=True, vmem_limit_bytes=60 * 2**20),
        name="sketch_products",
    )(inputs, query_inputs, w_gate, w_up, out_grads, query_grads, in_project, out_project, example_ids, query_ids)


def fused_local(n_tensor, *args):
    pairs, scores = sketch_products(n_tensor, *args)
    rank = args[8].shape[0]
    sketches = pairs.reshape(-1, rank // 2, 2, rank).transpose(0, 2, 1, 3).reshape(-1, rank * rank)
    return sketches, scores


def solution(mesh):
    n_tensor = mesh.shape["tensor"]
    paired = mesh.shape["groups"] == 2 and mesh.shape["dp"] == 4

    def local(*args):
        w_gate = args[6]
        if paired and w_gate.shape[1] % (2 * CHUNK) == 0:
            return fused_local(n_tensor, *args)
        return generic_local(*args)

    in_specs = (
        P(("groups", "dp"), "tensor"),
        P(("groups", "dp"), "tensor"),
        P(("groups", "dp"), None),
        P(("groups", "dp"), "tensor"),
        P(("groups", "dp"), "tensor"),
        P(("groups", "dp"), None),
        P("dp", "tensor"),
        P("dp", "tensor"),
        P(None, "tensor"),
        P(None, "tensor"),
    )
    out_specs = (P(("groups", "dp"), None), P(("groups", "dp"), None))
    return jax.shard_map(local, mesh=mesh, in_specs=in_specs, out_specs=out_specs, check_vma=False)
```

```python
import functools

import jax
import jax.numpy as jnp
from jax import lax
from jax.experimental import pallas as pl
from jax.experimental.pallas import tpu as pltpu
from jax.sharding import PartitionSpec as P

EX_DEV = 16
QEX_DEV = 16


def sketch_from(left, right, onehot):
    count = onehot.shape[1]
    spread = (onehot[:, :, None] * left[:, None, :]).reshape(left.shape[0], count * left.shape[1])
    return jnp.dot(spread.T, right, precision=lax.Precision.HIGHEST).reshape(
        count, left.shape[1] * right.shape[1]
    )


def member_table(ids, count):
    return (ids[:, None] == jnp.arange(count, dtype=jnp.int32)[None, :]).astype(jnp.float32)


def scores_from(projected, train_rows, rank, example_ids, query_ids):
    sketches = sketch_from(
        projected[:train_rows, :rank],
        projected[:train_rows, rank:],
        member_table(example_ids[0], EX_DEV),
    )
    query_part = projected[train_rows:]
    query_table = member_table(query_ids[0], QEX_DEV)
    local_sketch = sketch_from(query_part[:, :rank], query_part[:, rank:], query_table)
    query_sketches = lax.all_gather(local_sketch, "dp", axis=0, tiled=True)
    return sketches, scores_of(sketches, query_sketches, rank)


def scores_of(sketches, query_sketches, rank):
    train_norm = jnp.sqrt(jnp.sum(sketches * sketches, axis=1) + 1e-06)
    query_norm = jnp.sqrt(jnp.sum(query_sketches * query_sketches, axis=1) + 1e-06)
    inner = jnp.dot(sketches, query_sketches.T, precision=lax.Precision.HIGHEST)
    scores = rank * inner / (train_norm[:, None] * query_norm[None, :])
    return scores


def generic_local(
    inputs,
    out_grads,
    example_ids,
    query_inputs,
    query_grads,
    query_ids,
    w_gate,
    w_up,
    in_project,
    out_project,
):
    full_train, full_query = (
        lax.all_gather(inputs, "tensor", axis=1, tiled=True),
        lax.all_gather(query_inputs, "tensor", axis=1, tiled=True),
    )
    all_tokens = jnp.concatenate([full_train, full_query], 0)
    gate_act = jnp.dot(
        all_tokens,
        lax.all_gather(w_gate, "dp", axis=0, tiled=True),
        preferred_element_type=jnp.float32,
    )
    up_act = jnp.dot(
        all_tokens,
        lax.all_gather(w_up, "dp", axis=0, tiled=True),
        preferred_element_type=jnp.float32,
    )
    hidden = (jax.nn.silu(gate_act) * up_act).astype(jnp.bfloat16)
    all_grads = jnp.concatenate([out_grads, query_grads], 0)
    partial_sum = jnp.concatenate(
        [
            jnp.dot(all_grads, out_project.T, preferred_element_type=jnp.float32),
            jnp.dot(hidden, in_project.T, preferred_element_type=jnp.float32),
        ],
        1,
    )
    projected = lax.psum(partial_sum, "tensor")
    return scores_from(projected, inputs.shape[0], in_project.shape[0], example_ids, query_ids)


CHUNK = 256
MESH = pl.DeviceIdType.MESH


def sketch_kernel(
    n_tensor, chunks, x_ref, qx_ref, wg_ref, wu_ref, dy_ref, qdy_ref, proj_ref, oproj_ref, ids_ref, qids_ref,
    sketch_ref, scores_ref,
    tok, wts, grads, acc, lefts, swap, parts, terms, whole,
    spreads, grams, lqs, rqs, norms, idrows,
    lx, lw, zs, zr, ys, yr, xs, xr, ss, sr, fs, fr, lg, ls, lr, ps, pr, ts, tr, ws, wr, qs, qr, ns, nr, ds, dr, es, er,
):
    group = lax.axis_index("groups")
    dp = lax.axis_index("dp")
    me = lax.axis_index("tensor")
    train, cols = x_ref.shape
    rows = wg_ref.shape[0]
    base = group * (chunks * CHUNK)
    sibling = dp + 1 - 2 * (dp % 2)
    across = (dp + 2) % 4
    far = (sibling + 2) % 4

    def tok_at(slot, shard):
        return tok.at[slot, :, pl.ds(pl.multiple_of(shard * cols, cols), cols)]

    def wts_at(i, quarter):
        return wts.at[i, pl.ds(pl.multiple_of(quarter * rows, rows), rows), :]

    def z_copy(shard, way, to):
        return pltpu.make_async_remote_copy(
            tok_at(0, shard), tok_at(0, shard), zs.at[way, shard], zr.at[shard],
            device_id={"tensor": to}, device_id_type=MESH)

    def y_copy(shard):
        return pltpu.make_async_remote_copy(
            tok_at(0, shard), tok_at(1, shard), ys.at[shard], yr.at[shard],
            device_id={"groups": 1 - group}, device_id_type=MESH)

    def w_copy(i, quarter, send, recv, to):
        return pltpu.make_async_remote_copy(
            wts_at(i, quarter), wts_at(i, quarter), send.at[i], recv.at[i],
            device_id={"dp": to}, device_id_type=MESH)

    def local_w(i):
        columns = pl.ds(pl.multiple_of(base + i * CHUNK, CHUNK // 2), CHUNK)
        mine = pl.ds(pl.multiple_of(dp * rows, rows), rows)
        return (
            pltpu.make_async_copy(wg_ref.at[:, columns], wts.at[i, mine, pl.ds(0, CHUNK)], lw.at[0, i]),
            pltpu.make_async_copy(wu_ref.at[:, columns], wts.at[i, mine, pl.ds(CHUNK, CHUNK)], lw.at[1, i]),
        )

    own = pl.ds(pl.multiple_of(me * cols, cols), cols)
    local_x = (
        pltpu.make_async_copy(x_ref, tok.at[0, pl.ds(0, train), own], lx.at[0]),
        pltpu.make_async_copy(qx_ref, tok.at[0, pl.ds(train, qx_ref.shape[0]), own], lx.at[1]),
    )
    local_g = (
        pltpu.make_async_copy(dy_ref, grads.at[pl.ds(0, train)], lg.at[0]),
        pltpu.make_async_copy(qdy_ref, grads.at[pl.ds(train, qdy_ref.shape[0])], lg.at[1]),
    )
    for copy in local_x:
        copy.start()

    @pl.loop(0, chunks)
    def _(i):
        for copy in local_w(i):
            copy.start()

    barrier = pltpu.get_barrier_semaphore()
    targets = [{"groups": 1 - group}]
    targets += [{"dp": (dp + step) % 4} for step in range(1, 4)]
    targets += [{"tensor": (me + step) % n_tensor} for step in range(1, n_tensor)]
    for target in targets:
        pl.semaphore_signal(barrier, inc=1, device_id=target, device_id_type=MESH)
    for copy in local_g:
        copy.start()
    pl.semaphore_wait(barrier, len(targets))

    for copy in local_x:
        copy.wait()

    def pass_right(shard):
        @pl.when(me < n_tensor - 1)
        def _():
            z_copy(shard, 0, me + 1).start()

    def pass_left(shard):
        @pl.when(me > 0)
        def _():
            z_copy(shard, 1, me - 1).start()

    pass_right(me)
    pass_left(me)
    y_copy(me).start()

    @pl.loop(0, chunks)
    def _(i):
        for copy in local_w(i):
            copy.wait()
        w_copy(i, dp, xs, xr, across).start()
        w_copy(i, dp, ss, sr, sibling).start()

    acc[...] = jnp.zeros_like(acc)
    for copy in local_g:
        copy.wait()
    lefts[me] = lax.dot_general(
        oproj_ref[...], grads[...], (((1,), (1,)), ((), ())), preferred_element_type=jnp.float32)

    def hop(h):
        @pl.when(me >= h)
        def _():
            z_copy(me - h, 0, me).wait_recv()
            pass_right(me - h)
            y_copy(me - h).start()

        @pl.when(me + h < n_tensor)
        def _():
            z_copy(me + h, 1, me).wait_recv()
            pass_left(me + h)
            y_copy(me + h).start()

    def hand_on(i):
        w_copy(i, across, xs, xr, across).wait_recv()
        w_copy(i, across, fs, fr, sibling).start()

    def arrive(i):
        w_copy(i, sibling, ss, sr, sibling).wait_recv()
        w_copy(i, far, fs, fr, sibling).wait_recv()

    def finish(slot, i, both):
        gate, up = both[:, :CHUNK], both[:, CHUNK:]
        hidden = (gate / (1.0 + jnp.exp(-gate)) * up).astype(jnp.bfloat16)
        part = proj_ref[:, pl.ds(pl.multiple_of(base + i * CHUNK, CHUNK // 2), CHUNK)]
        acc[slot] += lax.dot_general(
            hidden, part, (((1,), (1,)), ((), ())), preferred_element_type=jnp.float32)

    def work(slot, i):
        finish(slot, i, jnp.dot(tok[slot], wts[i], preferred_element_type=jnp.float32))

    early = chunks // 2 + 1
    done = 0
    for h in range(1, n_tensor):
        upto = max(done, min(early, (early * h) // (n_tensor - 1)))
        for i in range(done, upto):
            hand_on(i)
        done = upto
        hop(h)

    def others():
        return [(me + step) % n_tensor for step in range(1, n_tensor)]

    def left_copy(source, to):
        return pltpu.make_async_remote_copy(
            lefts.at[source], lefts.at[source], ls.at[to], lr.at[source],
            device_id={"tensor": to}, device_id_type=MESH)

    def swap_copy():
        return pltpu.make_async_remote_copy(
            swap.at[0], swap.at[1], ps.at[0], pr.at[0], device_id={"groups": 1 - group}, device_id_type=MESH)

    def term_copy(source, to):
        return pltpu.make_async_remote_copy(
            parts.at[to], terms.at[source], ts.at[to], tr.at[source],
            device_id={"tensor": to}, device_id_type=MESH)

    def whole_copy(source, to):
        return pltpu.make_async_remote_copy(
            whole.at[source], whole.at[source], ws.at[to], wr.at[source],
            device_id={"tensor": to}, device_id_type=MESH)

    def dp_copy(buffer, send, recv, source, to):
        return pltpu.make_async_remote_copy(
            buffer.at[source], buffer.at[source], send.at[to], recv.at[source],
            device_id={"dp": to}, device_id_type=MESH)

    idrows[dp] = qids_ref[...]
    elsewhere = [(dp + step) % 4 for step in range(1, 4)]
    for to in elsewhere:
        dp_copy(idrows, ds, dr, dp, to).start()
    for to in others():
        left_copy(me, to).start()

    @pl.loop(0, chunks - 1)
    def _(i):
        @pl.when(i >= early)
        def _():
            hand_on(i)

        arrive(i)
        work(0, i)

    rank = proj_ref.shape[0]
    half = tok.shape[1] // 2
    for source in others():
        left_copy(source, source).wait_recv()
    left = lefts[0]
    for source in range(1, n_tensor):
        left = left + lefts[source]
    lqs[dp] = left[:, train:]
    dp_copy(lqs, es, er, dp, sibling).start()
    dp_copy(lqs, es, er, dp, across).start()

    def spread(left, ids, count, at, size):
        for side in range(2):
            some = left[side * (rank // 2):(side + 1) * (rank // 2)]
            top = some.astype(jnp.bfloat16).astype(jnp.float32)
            for k, piece in enumerate((top, some - top)):
                rows_of = [jnp.where(ids == e, piece, 0.0) for e in range(count)]
                spreads[k, side, :, pl.ds(at, size)] = jnp.concatenate(rows_of, axis=0).astype(jnp.bfloat16)

    spread(left[:, :train], ids_ref[...], EX_DEV, 0, train)
    spread(left[:, train:], qids_ref[...], QEX_DEV, train, left.shape[1] - train)
    def gram(k):
        grams[k] = lax.dot_general(
            left[:, :train], lqs[k], (((0,), (0,)), ((), ())),
            precision=lax.Precision.HIGHEST, preferred_element_type=jnp.float32)

    gram(dp)

    @pl.loop(0, n_tensor)
    def _(shard):
        y_copy(shard).wait_recv()

    @pl.loop(0, chunks - 1)
    def _(i):
        work(1, i)

    last = chunks - 1
    w_copy(last, sibling, ss, sr, sibling).wait_recv()

    hand_on(last)
    w_copy(last, far, fs, fr, sibling).wait_recv()

    def packed(slot):
        return jnp.concatenate([acc[slot, :half], acc[slot, half:]], axis=1)

    @pl.loop(0, 2)
    def _(turn):
        work(1 - turn, last)

        @pl.when(turn == 0)
        def _():
            swap[0] = packed(1)
            swap_copy().start()

    dp_copy(lqs, es, er, across, across).wait_recv()
    far_copy = pltpu.make_async_remote_copy(
        lqs.at[across], lqs.at[across], es.at[far], er.at[across],
        device_id={"dp": sibling}, device_id_type=MESH)
    far_copy.start()
    swap_copy().wait_recv()
    parts[...] = (packed(0) + swap[1]).reshape(parts.shape)
    for to in others():
        term_copy(me, to).start()
    total = parts[me]
    dp_copy(lqs, es, er, sibling, sibling).wait_recv()
    gram(sibling)
    gram(across)
    for source in others():
        term_copy(source, source).wait_recv()
        total = total + terms[source]
    whole[me] = total
    for to in others():
        whole_copy(me, to).start()
    dp_copy(lqs, es, er, far, far).wait_recv()
    gram(far)
    for source in others():
        whole_copy(source, source).wait_recv()
    both = whole[...].reshape(half, 2 * rank)
    right = jnp.concatenate([both[:, :rank], both[:, rank:]], axis=0)

    rqs[dp] = right[train:]
    for to in elsewhere:
        dp_copy(rqs, qs, qr, dp, to).start()

    def split(value):
        top = value.astype(jnp.bfloat16)
        return top, (value - top.astype(jnp.float32)).astype(jnp.bfloat16)

    def outer_sums(right, at):
        top, rest = split(right)
        pair = jnp.concatenate([top, rest], axis=1)
        sums = []
        for side in range(2):
            span = pl.ds(at, right.shape[0])
            first = jnp.dot(spreads[0, side, :, span], pair, preferred_element_type=jnp.float32)
            second = jnp.dot(spreads[1, side, :, span], top, preferred_element_type=jnp.float32)
            sums.append(first[:, :rank] + first[:, rank:] + second)
        return jnp.concatenate(sums, axis=1)

    own_queries = outer_sums(right[train:], train)
    across_lanes = lax.dot_general(
        jnp.ones((8, 2 * rank), jnp.float32), own_queries * own_queries, (((1,), (1,)), ((), ())),
        precision=lax.Precision.HIGHEST, preferred_element_type=jnp.float32)
    entries = own_queries.shape[0]
    query_of = lax.broadcasted_iota(jnp.int32, (entries, 128), 0) // (entries // QEX_DEV)
    place = lax.broadcasted_iota(jnp.int32, (entries, 128), 1)
    norms[dp] = jnp.dot(
        across_lanes, (query_of == place).astype(jnp.float32),
        precision=lax.Precision.HIGHEST, preferred_element_type=jnp.float32)
    for to in elsewhere:
        dp_copy(norms, ns, nr, dp, to).start()

    sketch = outer_sums(right[:train], 0)
    sketch_ref[...] = sketch
    squares = jnp.sum((sketch * sketch).reshape(EX_DEV, sketch.shape[0] // EX_DEV, 2 * rank), axis=1)
    train_norm = jnp.sqrt(jnp.sum(squares, axis=1, keepdims=True) + 1e-06)

    for source in elsewhere:
        dp_copy(rqs, qs, qr, source, source).wait_recv()
        dp_copy(idrows, ds, dr, source, source).wait_recv()
        dp_copy(norms, ns, nr, source, source).wait_recv()

    def table(ids, count):
        return (lax.broadcasted_iota(jnp.int32, (count, ids.shape[1]), 0) == ids).astype(jnp.float32)

    examples = table(ids_ref[...], EX_DEV).astype(jnp.bfloat16)
    top, rest = split(right[:train])
    mine = jnp.concatenate([top, rest, top], axis=1)
    found = []
    for k in range(4):
        top, rest = split(rqs[k])
        theirs = jnp.concatenate([top, top, rest], axis=1)
        gram = grams[k] * lax.dot_general(
            mine, theirs, (((1,), (1,)), ((), ())), preferred_element_type=jnp.float32)
        top, rest = split(gram)
        by_example = jnp.dot(examples, top, preferred_element_type=jnp.float32) + jnp.dot(
            examples, rest, preferred_element_type=jnp.float32)
        inner = lax.dot_general(
            by_example, table(idrows[k], QEX_DEV), (((1,), (1,)), ((), ())),
            precision=lax.Precision.HIGHEST, preferred_element_type=jnp.float32)
        query_norm = jnp.sqrt(norms[k][:1, :QEX_DEV] + 1e-06)
        found.append(rank * inner / (train_norm * query_norm))
    scores_ref[...] = jnp.concatenate(found, axis=1)

    for to in others():
        left_copy(me, to).wait_send()
        term_copy(me, to).wait_send()
        whole_copy(me, to).wait_send()
    swap_copy().wait_send()
    for to in elsewhere:
        dp_copy(rqs, qs, qr, dp, to).wait_send()
        dp_copy(idrows, ds, dr, dp, to).wait_send()
        dp_copy(norms, ns, nr, dp, to).wait_send()
    dp_copy(lqs, es, er, dp, sibling).wait_send()
    dp_copy(lqs, es, er, dp, across).wait_send()
    far_copy.wait_send()

    @pl.loop(0, chunks)
    def _(i):
        w_copy(i, dp, xs, xr, across).wait_send()
        w_copy(i, dp, ss, sr, sibling).wait_send()
        w_copy(i, across, fs, fr, sibling).wait_send()

    for shard in range(n_tensor):
        y_copy(shard).wait_send()

        @pl.when((shard <= me) & (me < n_tensor - 1))
        def _():
            z_copy(shard, 0, me).wait_send()

        @pl.when((shard >= me) & (me > 0))
        def _():
            z_copy(shard, 1, me).wait_send()


def sketch_products(
    n_tensor, inputs, out_grads, example_ids, query_inputs, query_grads, query_ids, w_gate, w_up, in_project, out_project
):
    tokens = inputs.shape[0] + query_inputs.shape[0]
    rank = in_project.shape[0]
    rows, units = w_gate.shape
    chunks = units // 2 // CHUNK
    anywhere = pl.BlockSpec(memory_space=pl.ANY)
    vmem = pl.BlockSpec(memory_space=pltpu.VMEM)
    dma = pltpu.SemaphoreType.DMA
    f32 = jnp.float32
    return pl.pallas_call(
        functools.partial(sketch_kernel, n_tensor, chunks),
        out_shape=(
            jax.ShapeDtypeStruct((EX_DEV * rank // 2, 2 * rank), f32),
            jax.ShapeDtypeStruct((EX_DEV, 4 * QEX_DEV), f32),
        ),
        in_specs=[anywhere] * 6 + [vmem] * 4,
        out_specs=(vmem, vmem),
        scratch_shapes=[
            pltpu.VMEM((2, tokens, inputs.shape[1] * n_tensor), jnp.bfloat16),
            pltpu.VMEM((chunks, rows * 4, 2 * CHUNK), jnp.bfloat16),
            pltpu.VMEM((tokens, out_grads.shape[1]), jnp.bfloat16),
            pltpu.VMEM((2, tokens, rank), f32),
            pltpu.VMEM((n_tensor, rank, tokens), f32),
            pltpu.VMEM((2, tokens // 2, 2 * rank), f32),
            pltpu.VMEM((n_tensor, tokens // 2 // n_tensor, 2 * rank), f32),
            pltpu.VMEM((n_tensor, tokens // 2 // n_tensor, 2 * rank), f32),
            pltpu.VMEM((n_tensor, tokens // 2 // n_tensor, 2 * rank), f32),
            pltpu.VMEM((2, 2, EX_DEV * rank // 2, tokens), jnp.bfloat16),
            pltpu.VMEM((4, inputs.shape[0], query_inputs.shape[0]), f32),
            pltpu.VMEM((4, rank, query_inputs.shape[0]), f32),
            pltpu.VMEM((4, query_inputs.shape[0], rank), f32),
            pltpu.VMEM((4, 8, 128), f32),
            pltpu.VMEM((4, 1, query_inputs.shape[0]), jnp.int32),
            dma((2,)), dma((2, chunks)), dma((2, n_tensor)), dma((n_tensor,)),
            dma((n_tensor,)), dma((n_tensor,)),
        ] + [dma((chunks,))] * 6 + [dma((2,))] + [dma((n_tensor,))] * 2 + [dma((1,))] * 2
        + [dma((n_tensor,))] * 4 + [dma((4,))] * 8,
        compiler_params=pltpu.CompilerParams(
            collective_id=0, has_side_effects=True, vmem_limit_bytes=60 * 2**20),
        name="sketch_products",
    )(inputs, query_inputs, w_gate, w_up, out_grads, query_grads, in_project, out_project, example_ids, query_ids)


def fused_local(n_tensor, *args):
    pairs, scores = sketch_products(n_tensor, *args)
    rank = args[8].shape[0]
    sketches = pairs.reshape(-1, rank // 2, 2, rank).transpose(0, 2, 1, 3).reshape(-1, rank * rank)
    return sketches, scores


def solution(mesh):
    n_tensor = mesh.shape["tensor"]
    paired = mesh.shape["groups"] == 2 and mesh.shape["dp"] == 4

    def local(*args):
        w_gate = args[6]
        if paired and w_gate.shape[1] % (2 * CHUNK) == 0:
            return fused_local(n_tensor, *args)
        return generic_local(*args)

    in_specs = (
        P(("groups", "dp"), "tensor"),
        P(("groups", "dp"), "tensor"),
        P(("groups", "dp"), None),
        P(("groups", "dp"), "tensor"),
        P(("groups", "dp"), "tensor"),
        P(("groups", "dp"), None),
        P("dp", "tensor"),
        P("dp", "tensor"),
        P(None, "tensor"),
        P(None, "tensor"),
    )
    out_specs = (P(("groups", "dp"), None), P(("groups", "dp"), None))
    return jax.shard_map(local, mesh=mesh, in_specs=in_specs, out_specs=out_specs, check_vma=False)
```
